128 devices in a mesh: section: 8 (over y_hi, x), tensor: 16 (over y_lo, z, core).
Axes of the slice: x: 4, y: 4 (y_hi: 2, y_lo: 2; y = y_hi * 2 + y_lo), z: 4, core: 2. Of those that a mesh axis runs over, the one named last changes fastest.
Arguments:
- incoming: bfloat16 [8, 3, 384, 8192], P('section', None, 'tensor'), may hold values from -6 to 6
- norm_gain: bfloat16 [8, 8192], P('section'), may hold values from 0.099609375 to 1.8984375
- w_query: bfloat16 [8, 8192, 8192], P('section', None, 'tensor'), may hold values from -0.0625 to 0.0625
- w_key_value: bfloat16 [8, 8192, 2, 1024], P('section', None, None, 'tensor'), may hold values from -0.0625 to 0.0625
- w_out: bfloat16 [8, 8192, 8192], P('section', 'tensor'), may hold values from -0.0625 to 0.0625
- kv_cache: bfloat16 [8, 2, 384, 1024], P('section'), may hold values from -1000 to 1000, as said below
- offsets: int32 [8, 3], P('section'), may hold values from 0 to 1152, as said below
Outputs:
- outgoing: bfloat16 [8, 3, 384, 8192], P('section', None, 'tensor')
The draws below stay inside these ranges and needn't reach their ends.
Inputs may be any that keep to these rules, and one draw needn't show every extreme that they name: offsets[s, j] = offsets[s, 0] + j * 384; offsets[s, 0] lies between 0 and 384, and is 0 at some section and 384 at another. `kv_cache`: cached keys are stored after the rotary embedding of their positions.
All inputs are finite; a program needn't handle non-finite values.
Results may differ from the reference program's by a relative error of at most 0.015.
Values may be sent and summed in bfloat16 or wider, within the bound.
No kernel may reach another device: no remote copies, remote signals or barrier semaphores. Data moves between devices by JAX's collectives and lax.ppermute only.
A program may use at most 128 MiB of HBM per device.

```python
import math
import jax
import jax.numpy as jnp
from jax import lax

D = 8192
QH = 64
KVH = 8
HD = 128
BLOCK = 384
SECTIONS = 8
CACHE = 384
N_TENSOR = 16


def draw_offsets(key, part):
    key = jax.random.fold_in(key, 7)
    start = jax.random.randint(jax.random.fold_in(key, 1), (SECTIONS,), 0, CACHE + 1).astype(jnp.int32)
    order = jax.random.permutation(jax.random.fold_in(key, 2), SECTIONS).astype(jnp.int32)
    start = start.at[order[0]].set(0)
    start = start.at[order[1]].set(CACHE)
    return (start[:, None] + BLOCK * jnp.arange(3, dtype=jnp.int32)[None, :]).astype(jnp.int32)


def draw_kv_cache(key, part):
    key = jax.random.fold_in(key, 11)
    shape = (SECTIONS, 2, CACHE, KVH * HD)
    return jnp.clip(jax.random.normal(key, shape, jnp.float32), -6.0, 6.0).astype(jnp.bfloat16)


def block_scale(own_key, dims, split, low, high):
    def one(dim, parts):
        steps = jax.random.uniform(jax.random.fold_in(jax.random.fold_in(own_key, 6), dim), (parts,), jnp.float32, low / len(split), high / len(split))
        return jnp.repeat(jnp.exp(steps), dims[dim] // parts).reshape((-1,) + (1,) * (len(dims) - dim - 1))

    loudness = one(*split[0])
    for cut in split[1:]:
        loudness = loudness * one(*cut)
    return loudness


def bell_draw(stream_key, shape, deviation, reach, cuts=(), kind=jnp.bfloat16):
    drawn = jax.random.normal(stream_key, shape, jnp.float32) * deviation
    if len(cuts) > 0:
        drawn = block_scale(stream_key, shape, cuts, -0.22, 0.18) * drawn
    return jnp.clip(drawn, min=-reach, max=reach).astype(kind)


def setup_inputs(seed: int = 0) -> dict:
    key_of = jax.random.split(jax.random.key(seed), 8)
    return {
        "incoming": bell_draw(key_of[0], (SECTIONS, 3, BLOCK, D), 1.0, 6.0, ((0, 8), (2, 16))),
        "norm_gain": jnp.clip(1.0 + 0.18 * jax.random.normal(key_of[1], (SECTIONS, D), jnp.float32), 0.099609375, 1.8984375).astype(jnp.bfloat16),
        "w_query": bell_draw(key_of[2], (SECTIONS, D, QH * HD), D ** -0.5, 0.0625, ((0, 8), (2, 16))),
        "w_key_value": bell_draw(key_of[3], (SECTIONS, D, 2, KVH * HD), D ** -0.5, 0.0625, ((0, 8), (3, 16))),
        "w_out": bell_draw(key_of[4], (SECTIONS, QH * HD, D), (QH * HD) ** -0.5, 0.0625, ((0, 8), (1, 16))),
        "kv_cache": draw_kv_cache(jax.random.fold_in(key_of[7], 71), 0),
        "offsets": draw_offsets(jax.random.fold_in(key_of[7], 71), 0),
    }


def rotary(values, position):
    half = values.shape[-1] // 2
    freq = 500000.0 ** (-jnp.arange(half, dtype=jnp.float32) * 2.0 / values.shape[-1])
    angle = position.astype(jnp.float32)[..., None, None] * freq
    cosine = jnp.cos(angle)
    sine = jnp.sin(angle)
    first = values[..., :half]
    second = values[..., half:]
    return jnp.concatenate([first * cosine - second * sine, second * cosine + first * sine], axis=-1)

def layer(handed, gain, w_query, w_key_value, w_out, cache, offset_row):
    widened = handed.astype(jnp.float32)
    normed = (widened * lax.rsqrt(lax.optimization_barrier(jnp.mean(widened * widened, axis=-1, keepdims=True)) + 1e-05) * gain.astype(jnp.float32)).astype(jnp.bfloat16)
    flat = normed.reshape(3 * BLOCK, D)
    position = offset_row[:, None] + jnp.arange(BLOCK, dtype=jnp.int32)[None, :]
    query = jnp.dot(flat, w_query, preferred_element_type=jnp.float32).reshape(3, BLOCK, QH, HD)
    query = rotary(query, position).astype(jnp.bfloat16)
    paired = jnp.dot(flat, w_key_value.reshape(D, 2 * KVH * HD), preferred_element_type=jnp.float32).astype(jnp.bfloat16)
    paired = paired.reshape(3, BLOCK, 2, KVH, HD)
    keys = rotary(paired[:, :, 0].astype(jnp.float32), position).astype(jnp.bfloat16).reshape(3 * BLOCK, KVH, HD)
    values = paired[:, :, 1].reshape(3 * BLOCK, KVH, HD)
    all_keys = jnp.concatenate([cache[0].reshape(CACHE, KVH, HD), keys], axis=0).astype(jnp.float32)
    all_values = jnp.concatenate([cache[1].reshape(CACHE, KVH, HD), values], axis=0).astype(jnp.float32)
    slots = jnp.arange(CACHE, dtype=jnp.int32)
    key_position = jnp.concatenate([slots, position.reshape(-1)])
    key_ok = jnp.concatenate([slots < offset_row[0], jnp.ones((3 * BLOCK,), dtype=bool)])
    scale = 1.0 / math.sqrt(HD)
    width = QH * HD // N_TENSOR
    results = []
    for which in range(3):
        grouped = query[which].reshape(BLOCK, KVH, QH // KVH, HD).astype(jnp.float32)
        scores = jnp.einsum('cngd,knd->ngck', grouped, all_keys) * scale
        allowed = (key_position[None, :] <= position[which][:, None]) & key_ok[None, :]
        scores = jnp.where(allowed[None, None], scores, -1e+30)
        weights = jax.nn.softmax(scores, axis=-1).astype(jnp.bfloat16)
        attended = jnp.einsum('ngck,knd->cngd', weights.astype(jnp.float32), all_values)
        attended = attended.astype(jnp.bfloat16).reshape(BLOCK, QH * HD)
        total = jnp.zeros((BLOCK, D), jnp.float32)
        for group_index in range(N_TENSOR):
            term = jnp.dot(attended[:, group_index * width:(group_index + 1) * width], w_out[group_index * width:(group_index + 1) * width], preferred_element_type=jnp.float32).astype(jnp.bfloat16)
            term = lax.optimization_barrier(term).astype(jnp.float32)
            total = total + term
        results.append((widened[which] + total).astype(jnp.bfloat16))
    return jnp.stack(results)

def reference(incoming, norm_gain, w_query, w_key_value, w_out, kv_cache, offsets):
    handed_all = jnp.roll(incoming, 1, axis=0)
    outputs = []
    for section_index in range(SECTIONS):
        outputs.append(layer(handed_all[section_index], norm_gain[section_index], w_query[section_index], w_key_value[section_index], w_out[section_index], kv_cache[section_index], offsets[section_index]))
    return jnp.stack(outputs)
```

```python
import functools
import math

import jax
import jax.numpy as jnp
from jax import lax
from jax.experimental import pallas as pl
from jax.experimental.pallas import tpu as pltpu
from jax.sharding import PartitionSpec as P

HD = 128
BLOCK = 384
CACHE = 384
D = 8192
HALF = D // 2
NZ = 4
ROWS = 192
PIECE = 48
K_CHUNK = 1024
N_CHUNK = 1024
SLOTS = (0, -1, 1, 2)


def tensor_index(y, z, c):
    return (y * NZ + z % NZ) * 2 + c


def move(value, dy=0, dz=0, dc=0):
    pairs = []
    for y in range(2):
        for z in range(NZ):
            for c in range(2):
                pairs.append((tensor_index(y, z, c), tensor_index(y ^ dy, z + dz, c ^ dc)))
    return lax.ppermute(value, "tensor", pairs)


def from_behind(value, axis, by):
    devices = lax.axis_size(axis)
    return lax.ppermute(value, axis, [(i, (i + by) % devices) for i in range(devices)])


def normalize(handed, gain):
    widened = handed.astype(jnp.float32)
    return (
        widened
        * lax.rsqrt(jnp.mean(widened * widened, axis=-1, keepdims=True) + 1e-05)
        * gain.astype(jnp.float32)
    ).astype(jnp.bfloat16)


def project_kernel(
    core, own, left, right, far_a, far_b, wq_mine, wq_other, wkv_mine, wkv_other, cosine, sine,
    query, kv, acc_q, acc_kv,
):
    step = pl.program_id(0)
    steps = pl.num_programs(0)
    far = jnp.where(step < steps // 2, far_a[...], far_b[...])
    x = jnp.concatenate([own[...], left[...], right[...], far], axis=0)

    @pl.when(step == 0)
    def _():
        acc_q[...] = jnp.zeros_like(acc_q)
        acc_kv[...] = jnp.zeros_like(acc_kv)

    for half, (wq, wkv) in enumerate(((wq_mine, wkv_mine), (wq_other, wkv_other))):
        acc_q[:, half * 512 : half * 512 + 512] += jnp.dot(
            x, wq[...], preferred_element_type=jnp.float32
        )
        acc_kv[:, half * HD : half * HD + HD] += jnp.dot(
            x, wkv[...], preferred_element_type=jnp.float32
        )

    @pl.when(step == steps - 1)
    def _():
        cos = cosine[...]
        sin = sine[...]

        def turn(u):
            return u * cos + pltpu.roll(u, HD // 2, 1) * sin

        for head in range(8):
            query[head] = turn(acc_q[:, head * HD : head * HD + HD]).astype(jnp.bfloat16)
        mine = acc_kv[:, :HD]
        other = acc_kv[:, HD:]
        first = core[0] == 0
        low = jnp.where(first, mine, other)
        high = jnp.where(first, other, mine)
        lower = lax.broadcasted_iota(jnp.int32, (ROWS, HD), 1) < HD // 2
        keys = jnp.where(lower, low, pltpu.roll(high, HD // 2, 1))
        values = jnp.where(lower, pltpu.roll(low, HD // 2, 1), high)
        keys = keys.astype(jnp.bfloat16).astype(jnp.float32)
        kv[0] = turn(keys).astype(jnp.bfloat16)
        kv[1] = values.astype(jnp.bfloat16)


def project(core, pieces, weights, cosine, sine):
    steps = D // K_CHUNK
    near = pl.BlockSpec((PIECE, K_CHUNK), lambda k, c: (0, k))
    specs = [near, near, near]
    specs.append(pl.BlockSpec((PIECE, K_CHUNK), lambda k, c: (0, jnp.minimum(k, steps // 2 - 1))))
    specs.append(pl.BlockSpec((PIECE, K_CHUNK), lambda k, c: (0, jnp.maximum(k - steps // 2, 0))))
    for w in weights:
        specs.append(pl.BlockSpec((K_CHUNK, w.shape[1]), lambda k, c: (k, 0)))
    table = pl.BlockSpec((ROWS, HD), lambda k, c: (0, 0))
    specs += [table, table]
    return pl.pallas_call(
        project_kernel,
        out_shape=(
            jax.ShapeDtypeStruct((8, ROWS, HD), jnp.bfloat16),
            jax.ShapeDtypeStruct((2, ROWS, HD), jnp.bfloat16),
        ),
        grid_spec=pltpu.PrefetchScalarGridSpec(
            num_scalar_prefetch=1,
            grid=(steps,),
            in_specs=specs,
            out_specs=(
                pl.BlockSpec((8, ROWS, HD), lambda k, c: (0, 0, 0)),
                pl.BlockSpec((2, ROWS, HD), lambda k, c: (0, 0, 0)),
            ),
            scratch_shapes=[
                pltpu.VMEM((ROWS, 1024), jnp.float32),
                pltpu.VMEM((ROWS, 2 * HD), jnp.float32),
            ],
        ),
        compiler_params=pltpu.CompilerParams(vmem_limit_bytes=40 * 2**20),
        cost_estimate=pl.CostEstimate(
            flops=2 * ROWS * D * 1280, bytes_accessed=24 * 2**20, transcendentals=0
        ),
        name="project",
    )(core, *pieces, *weights, cosine, sine)


def attend_kernel(blocks, scalars, query, cache, q_place, k_place, *refs):
    windows = refs[: 2 * blocks]
    wo_mine, wo_other = refs[2 * blocks : 2 * blocks + 2]
    own, minus, plus, far_a, far_b = refs[2 * blocks + 2 : 2 * blocks + 7]
    attended, wo, sems = refs[2 * blocks + 7 :]
    step = pl.program_id(0)
    steps = pl.num_programs(0)

    def fetch(n, half):
        source = (wo_mine, wo_other)[half]
        return pltpu.make_async_copy(
            source.at[:, pl.ds(pl.multiple_of(n * N_CHUNK, N_CHUNK), N_CHUNK)],
            wo.at[n, pl.ds(half * 512, 512), :],
            sems.at[n, half],
        )

    @pl.when(step == 0)
    def _():
        for n in range(D // N_CHUNK):
            fetch(n, 0).start()
            fetch(n, 1).start()
        scale = math.log2(math.e) / math.sqrt(HD)
        slot = lax.broadcasted_iota(jnp.int32, (1, CACHE), 1)
        cache_bias = jnp.where(slot < scalars[1], 0.0, -1e30)
        causal_bias = jnp.where(k_place[...] <= q_place[...], 0.0, -1e30)
        keys = [cache[0]] + [w[0] for w in windows]
        values = [cache[1]] + [w[1] for w in windows]
        keys = jnp.concatenate(keys, axis=0)
        values = jnp.concatenate(values, axis=0)
        before = CACHE + (blocks - 1) * BLOCK
        for head in range(8):
            scores = lax.dot_general(
                query[head], keys, (((1,), (1,)), ((), ())), preferred_element_type=jnp.float32
            )
            parts = [scores[:, :CACHE] + cache_bias]
            if blocks > 1:
                parts.append(scores[:, CACHE:before])
            parts.append(scores[:, before:] + causal_bias)
            scores = jnp.concatenate(parts, axis=1)
            top = jnp.max(scores, axis=1, keepdims=True)
            grown = jnp.exp2((scores - top) * scale)
            total = jnp.sum(grown, axis=1, keepdims=True)
            out = jnp.dot(grown.astype(jnp.bfloat16), values, preferred_element_type=jnp.float32)
            attended[:, head * HD : head * HD + HD] = (out / total).astype(jnp.bfloat16)

    fetch(step, 0).wait()
    fetch(step, 1).wait()
    term = jnp.dot(attended[...], wo[step], preferred_element_type=jnp.float32).astype(jnp.bfloat16)
    own[...] = term[:PIECE]
    minus[...] = term[PIECE : 2 * PIECE]
    plus[...] = term[2 * PIECE : 3 * PIECE]

    @pl.when(step < steps // 2)
    def _():
        far_a[...] = term[3 * PIECE :]

    @pl.when(step >= steps // 2)
    def _():
        far_b[...] = term[3 * PIECE :]


def attend(scalars, query, cache, q_place, k_place, windows, wo_mine, wo_other):
    steps = D // N_CHUNK
    blocks = len(windows) // 2
    whole = lambda a: pl.BlockSpec(a.shape, lambda n, s: (0,) * a.ndim)
    specs = [
        whole(query),
        pl.BlockSpec((2, CACHE, HD), lambda n, s: (0, 0, s[0])),
        whole(q_place),
        whole(k_place),
        *[whole(w) for w in windows],
        pl.BlockSpec(memory_space=pl.ANY),
        pl.BlockSpec(memory_space=pl.ANY),
    ]
    near = pl.BlockSpec((PIECE, N_CHUNK), lambda n, s: (0, n))
    full = jax.ShapeDtypeStruct((PIECE, D), jnp.bfloat16)
    half = jax.ShapeDtypeStruct((PIECE, HALF), jnp.bfloat16)
    keys = CACHE + blocks * BLOCK
    return pl.pallas_call(
        functools.partial(attend_kernel, blocks),
        out_shape=(full, full, full, half, half),
        grid_spec=pltpu.PrefetchScalarGridSpec(
            num_scalar_prefetch=1,
            grid=(steps,),
            in_specs=specs,
            out_specs=(
                near,
                near,
                near,
                pl.BlockSpec((PIECE, N_CHUNK), lambda n, s: (0, jnp.minimum(n, steps // 2 - 1))),
                pl.BlockSpec((PIECE, N_CHUNK), lambda n, s: (0, jnp.maximum(n - steps // 2, 0))),
            ),
            scratch_shapes=[
                pltpu.VMEM((ROWS, 1024), jnp.bfloat16),
                pltpu.VMEM((steps, 1024, N_CHUNK), jnp.bfloat16),
                pltpu.SemaphoreType.DMA((steps, 2)),
            ],
        ),
        compiler_params=pltpu.CompilerParams(vmem_limit_bytes=52 * 2**20),
        cost_estimate=pl.CostEstimate(
            flops=2 * ROWS * D * 1024 + 4 * 8 * ROWS * keys * HD,
            bytes_accessed=21 * 2**20,
            transcendentals=8 * ROWS * keys,
        ),
        name="attend",
    )(scalars, query, cache, q_place, k_place, *windows, wo_mine, wo_other)


def shards(incoming, norm_gain, w_query, w_key_value, w_out, kv_cache, offsets):
    index = lax.axis_index("tensor")
    core = index % 2
    z = index // 2 % NZ
    y = index // (2 * NZ)
    head = index // 2
    offset = offsets[0, 0]
    handed = [from_behind(incoming[0, which], "section", 1) for which in range(3)]

    wkv = w_key_value[0].reshape(D, 2 * w_key_value.shape[3])
    wq = w_query[0]
    wo = w_out[0]
    wq_other = move(wq, dc=1)
    wkv_other = move(wkv, dc=1)
    wo_other = move(wo, dc=1)
    weights = (wq, wq_other, wkv, wkv_other)

    within = jnp.arange(24, dtype=jnp.int32)

    def places(c):
        return jnp.concatenate(
            [tensor_index(y ^ dy, z + dz, c) * 24 + within for dz in SLOTS for dy in range(2)]
        )

    mine = places(core)
    other = places(1 - core)
    q_place = mine[:, None]
    k_place = jnp.concatenate([mine, other])[None, :]
    freq = 500000.0 ** (-jnp.arange(HD // 2, dtype=jnp.float32) * 2.0 / HD)
    cosines = []
    sines = []
    for which in range(3):
        angle = (offsets[0, which] + mine).astype(jnp.float32)[:, None] * freq
        cos = jnp.cos(angle)
        sin = jnp.sin(angle)
        cosines.append(jnp.concatenate([cos, cos], axis=1))
        sines.append(jnp.concatenate([-sin, sin], axis=1))
    core_scalar = core.reshape(1)
    scalars = jnp.stack([head, offset])
    cache = kv_cache[0]

    windows = []
    results = []
    for which in range(3):
        normed = normalize(handed[which], norm_gain[0])
        own = jnp.concatenate([normed, move(normed, dy=1)], axis=0)
        left = move(own, dz=1)
        right = move(own, dz=-1)
        far_a = move(left[:, :HALF], dz=1)
        far_b = move(right[:, HALF:], dz=-1)
        query, kv = project(
            core_scalar, (own, left, right, far_a, far_b), weights, cosines[which], sines[which]
        )
        windows += [kv, move(kv, dc=1)]
        own, minus, plus, far_a, far_b = attend(
            scalars, query, cache, q_place, k_place, tuple(windows), wo, wo_other
        )
        far_a = move(far_a, dz=1)
        far_b = move(far_b, dz=-1)
        f32 = lambda a: a.astype(jnp.float32)
        plus = jnp.concatenate(
            [(f32(plus[:, :HALF]) + f32(far_a)).astype(jnp.bfloat16), plus[:, HALF:]], axis=1
        )
        minus = jnp.concatenate(
            [minus[:, :HALF], (f32(minus[:, HALF:]) + f32(far_b)).astype(jnp.bfloat16)], axis=1
        )
        summed = f32(own) + f32(move(plus, dz=1)) + f32(move(minus, dz=-1))
        passed = move(summed[24:].astype(jnp.bfloat16), dy=1)
        results.append(
            (f32(handed[which]) + summed[:24] + f32(passed)).astype(jnp.bfloat16)
        )
    return jnp.stack(results)[None]


def solution(mesh):
    placed = (
        P("section", None, "tensor", None),
        P("section", None),
        P("section", None, "tensor"),
        P("section", None, None, "tensor"),
        P("section", "tensor", None),
        P("section", None, None, None),
        P("section", None),
    )
    return jax.shard_map(
        shards,
        mesh=mesh,
        in_specs=placed,
        out_specs=P("section", None, "tensor", None),
        check_vma=False,
    )
```

```python
import functools
import math

import jax
import jax.numpy as jnp
from jax import lax
from jax.experimental import pallas as pl
from jax.experimental.pallas import tpu as pltpu
from jax.sharding import PartitionSpec as P

HD = 128
BLOCK = 384
CACHE = 384
D = 8192
NZ = 4
SHARD = 24
ROWS = 192
K_CHUNK = 2048
N_CHUNK = 2048
PROJECT_COST = (12,12,12)
ATTEND_COST = (0,12,12)
Y, A, B = (1, 0), (0, 1), (0, 3)

HALF = D // 2
PIECE = 2 * SHARD

ORDER_IN = (Y, A, B)
SCATTER = (
    ((0, 8192, (A, B, Y)),),
    ((0, 4096, (B, Y, A)), (4096, 4096, (A, B, Y)),),
    ((0, 4096, (Y, A, B)), (4096, 4096, (A, B, Y)),),
)


def steps_to(order, block):
    y = z = 0
    for bit in range(3):
        if block >> bit & 1:
            y ^= order[bit][0]
            z ^= order[bit][1]
    return y, z


def reorder(source, target):
    known = [steps_to(source, block) for block in range(8)]
    return [known.index(steps_to(target, block)) for block in range(8)]


def tensor_index(y, z, c):
    return (y * NZ + z) * 2 + c


def move(value, step=(0, 0), dc=0):
    pairs = []
    for y in range(2):
        for z in range(NZ):
            for c in range(2):
                pairs.append((tensor_index(y, z, c), tensor_index(y ^ step[0], z ^ step[1], c ^ dc)))
    return lax.ppermute(value, "tensor", pairs)


def from_behind(value, dy=0):
    sections = lax.axis_size("section")
    tensors = 4 * NZ
    pairs = []
    for s in range(sections):
        for t in range(tensors):
            target = (s + 1) % sections * tensors + (t ^ dy * 2 * NZ)
            pairs.append((s * tensors + t, target))
    return lax.ppermute(value, ("section", "tensor"), pairs)


ANY = pl.BlockSpec(memory_space=pl.ANY)


def params(mib):
    return pltpu.CompilerParams(vmem_limit_bytes=mib * 2**20)


def cost(giga=0):
    return pl.CostEstimate(flops=giga * 10**9, bytes_accessed=0, transcendentals=0)


def bf16(*shape):
    return jax.ShapeDtypeStruct(shape, jnp.bfloat16)


def f32(*shape):
    return jax.ShapeDtypeStruct(shape, jnp.float32)


def wide(ref):
    return ref[...].astype(jnp.float32)


def full_spec(shape):
    return pl.BlockSpec(shape, lambda i, n=len(shape): (0,) * n)


def small(kernel, ins, outs, after, name, mib=16):
    picked = [isinstance(a, tuple) for a in ins]
    specs = [
        pl.BlockSpec((None, SHARD, D), lambda i, which=a[1]: (which, 0, 0))
        if is_picked
        else full_spec(a.shape)
        for a, is_picked in zip(ins, picked)
    ]
    ins = [a[0] if is_picked else a for a, is_picked in zip(ins, picked)]

    def body(*refs):
        kernel(refs[: len(ins)], refs[len(ins) + len(after) : -1])
        refs[-1][...] = jnp.zeros((8, 128), jnp.float32)

    outs = list(outs) + [f32(8, 128)]
    *results, token = pl.pallas_call(
        body,
        grid=(1,),
        in_specs=specs + [ANY] * len(after),
        out_specs=[full_spec(o.shape) for o in outs],
        out_shape=outs,
        compiler_params=params(mib),
        cost_estimate=cost(),
        name=name,
    )(*ins, *after)
    return results, (token,)


def norm(mine, other, gain, after):
    def kernel(ins, outs):
        rows = jnp.concatenate([wide(ins[0]), wide(ins[1])], axis=0)
        mean = jnp.mean(rows * rows, axis=1, keepdims=True)
        outs[0][...] = (rows * lax.rsqrt(mean + 1e-05) * wide(ins[2])).astype(jnp.bfloat16)

    return small(kernel, (mine, other, gain), [bf16(PIECE, D)], after, "norm")


def parts(over_a, over_b, after):
    def kernel(ins, outs):
        outs[0][...] = ins[0][:, :HALF]
        outs[1][...] = ins[1][:, HALF:]

    return small(kernel, (over_a, over_b), [bf16(PIECE, HALF)] * 2, after, "parts")


def halve(kept, received, after, base=None, lanes=()):
    def kernel(ins, outs):
        for lane in range(len(kept)):
            rows = wide(ins[2 * lane]) + wide(ins[2 * lane + 1])
            half = rows.shape[0] // 2
            keep = rows[:half]
            if base is not None:
                start, width, _ = lanes[lane]
                keep = keep + ins[-1][:, start : start + width].astype(jnp.float32)
            outs[2 * lane][...] = keep
            outs[2 * lane + 1][...] = rows[half:].astype(jnp.bfloat16)

    ins = [a for pair in zip(kept, received) for a in pair]
    if base is not None:
        ins.append(base)
    outs = []
    for a in kept:
        half = (a.shape[0] // 2, a.shape[1])
        outs += [f32(*half), bf16(*half)]
    results, token = small(kernel, ins, outs, after, "halve")
    return results[0::2], results[1::2], token


def project_kernel(
    own, over_a, over_b, far_a, far_b, wq_mine, wq_other, wkv_mine, wkv_other, cosine, sine, flag, *refs
):
    query, kv, acc_q, acc_kv = refs[-4:]
    step = pl.program_id(0)
    steps = pl.num_programs(0)
    far = jnp.where(step < steps // 2, far_a[...], far_b[...])
    x = jnp.concatenate([own[...], over_a[...], over_b[...], far], axis=0)

    @pl.when(step == 0)
    def _():
        acc_q[...] = jnp.zeros_like(acc_q)
        acc_kv[...] = jnp.zeros_like(acc_kv)

    for half, (wq, wkv) in enumerate(((wq_mine, wkv_mine), (wq_other, wkv_other))):
        acc_q[:, half * 512 : half * 512 + 512] += jnp.dot(
            x, wq[...], preferred_element_type=jnp.float32
        )
        acc_kv[:, half * HD : half * HD + HD] += jnp.dot(
            x, wkv[...], preferred_element_type=jnp.float32
        )

    @pl.when(step == steps - 1)
    def _():
        cos = cosine[...]
        sin = sine[...]

        def turn(u):
            return u * cos + pltpu.roll(u, HD // 2, 1) * sin

        for head in range(8):
            query[head] = turn(acc_q[:, head * HD : head * HD + HD]).astype(jnp.bfloat16)
        first = flag[...] == 0
        mine = acc_kv[:, :HD]
        other = acc_kv[:, HD:]
        low = jnp.where(first, mine, other)
        high = jnp.where(first, other, mine)
        lower = lax.broadcasted_iota(jnp.int32, (ROWS, HD), 1) < HD // 2
        keys = jnp.where(lower, low, pltpu.roll(high, HD // 2, 1))
        values = jnp.where(lower, pltpu.roll(low, HD // 2, 1), high)
        keys = keys.astype(jnp.bfloat16).astype(jnp.float32)
        kv[0] = turn(keys).astype(jnp.bfloat16)
        kv[1] = values.astype(jnp.bfloat16)


def lane_spec(start, width, chunk):
    first = start // chunk
    count = width // chunk
    return pl.BlockSpec(
        (ROWS // 2, chunk), lambda k, *_: (0, jnp.clip(k - first, 0, count - 1))
    )


def project(which, pieces, weights, cosine, sine, flag, after):
    steps = D // K_CHUNK
    near = pl.BlockSpec((PIECE, K_CHUNK), lambda k: (0, k))
    specs = [near, near, near]
    specs.append(pl.BlockSpec((PIECE, K_CHUNK), lambda k: (0, jnp.minimum(k, steps // 2 - 1))))
    specs.append(pl.BlockSpec((PIECE, K_CHUNK), lambda k: (0, jnp.maximum(k - steps // 2, 0))))
    for w in weights:
        specs.append(pl.BlockSpec((K_CHUNK, w.shape[1]), lambda k: (k, 0)))
    table = pl.BlockSpec((None, ROWS, HD), lambda k: (which, 0, 0))
    specs += [table, table, full_spec(flag.shape)] + [ANY] * len(after)
    return pl.pallas_call(
        project_kernel,
        out_shape=(bf16(8, ROWS, HD), bf16(2, ROWS, HD)),
        grid=(steps,),
        in_specs=specs,
        out_specs=(
            pl.BlockSpec((8, ROWS, HD), lambda k: (0, 0, 0)),
            pl.BlockSpec((2, ROWS, HD), lambda k: (0, 0, 0)),
        ),
        scratch_shapes=[
            pltpu.VMEM((ROWS, 1024), jnp.float32),
            pltpu.VMEM((ROWS, 2 * HD), jnp.float32),
        ],
        compiler_params=params(44),
        cost_estimate=cost(PROJECT_COST[which]),
        name="project",
    )(*pieces, *weights, cosine, sine, flag, *after)


def attend_kernel(blocks, order, lanes, scalars, query, cache, q_place, k_place, *refs):
    windows = refs[:blocks]
    weights = refs[blocks : blocks + 2]
    count = 2 * len(lanes)
    outs = refs[-5 - count : -5]
    token, raw, attended, wo, sems = refs[-5:]
    step = pl.program_id(0)

    def fetch(n, half):
        return pltpu.make_async_copy(
            weights[half].at[:, pl.ds(pl.multiple_of(n * N_CHUNK, N_CHUNK), N_CHUNK)],
            wo.at[n, pl.ds(half * 512, 512), :],
            sems.at[n, half],
        )

    @pl.when(step == 0)
    def _():
        for n in range(D // N_CHUNK):
            fetch(n, 0).start()
            fetch(n, 1).start()
        token[...] = jnp.zeros((8, 128), jnp.float32)
        scale = math.log2(math.e) / math.sqrt(HD)
        slot = lax.broadcasted_iota(jnp.int32, (1, CACHE), 1)
        cache_bias = jnp.where(slot < scalars[1], 0.0, -1e30)
        causal_bias = jnp.where(k_place[...] <= q_place[...], 0.0, -1e30)
        keys = jnp.concatenate([cache[0]] + [w[c, 0] for w in windows for c in range(2)], axis=0)
        values = jnp.concatenate([cache[1]] + [w[c, 1] for w in windows for c in range(2)], axis=0)
        before = CACHE + (blocks - 1) * BLOCK
        for head in range(8):
            scores = lax.dot_general(
                query[head], keys, (((1,), (1,)), ((), ())), preferred_element_type=jnp.float32
            )
            parts = [scores[:, :CACHE] + cache_bias]
            if blocks > 1:
                parts.append(scores[:, CACHE:before])
            parts.append(scores[:, before:] + causal_bias)
            scores = jnp.concatenate(parts, axis=1)
            top = jnp.max(scores, axis=1, keepdims=True)
            grown = jnp.exp2((scores - top) * scale)
            total = jnp.sum(grown, axis=1, keepdims=True)
            out = jnp.dot(grown.astype(jnp.bfloat16), values, preferred_element_type=jnp.float32)
            raw[:, head * HD : head * HD + HD] = out / total
        for lane, (_, _, target) in enumerate(lanes):
            places = reorder(order, target)
            rows = [raw[p * SHARD : p * SHARD + SHARD] for p in places]
            attended[lane] = jnp.concatenate(rows, axis=0).astype(jnp.bfloat16)

    fetch(step, 0).wait()
    fetch(step, 1).wait()
    for lane, (start, width, _) in enumerate(lanes):
        first, last = start // N_CHUNK, (start + width) // N_CHUNK - 1

        @pl.when(jnp.logical_and(step >= first, step <= last))
        def _(lane=lane):
            term = jnp.dot(attended[lane], wo[step], preferred_element_type=jnp.float32)
            term = term.astype(jnp.bfloat16)
            outs[2 * lane][...] = term[: ROWS // 2]
            outs[2 * lane + 1][...] = term[ROWS // 2 :]


def attend(order, lanes, scalars, query, cache, q_place, k_place, windows, wo, after):
    steps = D // N_CHUNK
    blocks = len(windows)
    whole = lambda a: pl.BlockSpec(a.shape, lambda n, s: (0,) * a.ndim)
    specs = [
        whole(query),
        pl.BlockSpec((2, CACHE, HD), lambda n, s: (0, 0, s[0])),
        whole(q_place),
        whole(k_place),
        *[whole(w) for w in windows],
        ANY,
        ANY,
        *[ANY] * len(after),
    ]
    out_shape = []
    out_specs = []
    for start, width, _ in lanes:
        out_shape += [bf16(ROWS // 2, width)] * 2
        out_specs += [lane_spec(start, width, N_CHUNK)] * 2
    *results, token = pl.pallas_call(
        functools.partial(attend_kernel, blocks, order, lanes),
        out_shape=(*out_shape, f32(8, 128)),
        grid_spec=pltpu.PrefetchScalarGridSpec(
            num_scalar_prefetch=1,
            grid=(steps,),
            in_specs=specs,
            out_specs=(*out_specs, pl.BlockSpec((8, 128), lambda n, s: (0, 0))),
            scratch_shapes=[
                pltpu.VMEM((ROWS, 1024), jnp.float32),
                pltpu.VMEM((len(lanes), ROWS, 1024), jnp.bfloat16),
                pltpu.VMEM((steps, 1024, N_CHUNK), jnp.bfloat16),
                pltpu.SemaphoreType.DMA((steps, 2)),
            ],
        ),
        compiler_params=params(48),
        cost_estimate=cost(ATTEND_COST[blocks - 1]),
        name="attend",
    )(scalars, query, cache, q_place, k_place, *windows, *wo, *after)
    return results[0::2], results[1::2], (token,)


def shards(incoming, norm_gain, w_query, w_key_value, w_out, kv_cache, offsets):
    index = lax.axis_index("tensor")
    core = index % 2
    z = index // 2 % NZ
    y = index // (2 * NZ)
    head = index // 2
    offset = offsets[0, 0]
    handed = []
    beside = []
    for b in range(3):
        handed.append((from_behind(incoming[0, b : b + 1]), 0))
        beside.append((from_behind(incoming[0, b : b + 1], 1), 0))
    pairs = [[i, i + 1] for i in range(0, 4 * NZ, 2)]
    share = lambda a: lax.all_gather(a, "tensor", axis_index_groups=pairs)
    wkv = w_key_value[0].reshape(D, 2 * w_key_value.shape[3])
    wq_other = move(w_query[0], dc=1)
    wkv_other = move(wkv, dc=1)
    wo_other = move(w_out[0], dc=1)
    weights = (w_query[0], wq_other, wkv, wkv_other)
    arrived = (wq_other[:8, :128], wkv_other[:8, :128])
    flag = jnp.full((1, HD), core, jnp.int32)

    within = jnp.arange(SHARD, dtype=jnp.int32)
    freq = 500000.0 ** (-jnp.arange(HD // 2, dtype=jnp.float32) * 2.0 / HD)
    def places(c):
        moves = [steps_to(ORDER_IN, block) for block in range(8)]
        return jnp.concatenate(
            [tensor_index(y ^ dy, z ^ dz, c) * SHARD + within for dy, dz in moves]
        )

    mine = places(core)
    q_place = mine[:, None]
    k_place = jnp.concatenate([places(0), places(1)])[None, :]
    position = (offsets[0][:, None] + mine[None, :]).astype(jnp.float32)
    angle = position[:, :, None] * freq
    cos = jnp.cos(angle)
    sin = jnp.sin(angle)
    cosines = jnp.concatenate([cos, cos], axis=2)
    sines = jnp.concatenate([-sin, sin], axis=2)
    scalars = jnp.stack([head, offset])
    cache = kv_cache[0]

    held = [None] * 3
    sent = [None] * 3
    queries = [None] * 3
    windows = []
    results = [None] * 3

    def send(b, lanes, values, bit):
        sent[b] = [move(a, lane[2][bit]) for a, lane in zip(values, lanes)]

    own = [None] * 3
    near = [None] * 3
    far = [None] * 3

    def start_block(b, after):
        (own[b],), token = norm(handed[b], beside[b], norm_gain, after)
        near[b] = (move(own[b], A), move(own[b], B))
        return token

    def grow(b, after):
        (over_a, over_b), token = parts(*near[b], after)
        far[b] = (move(over_a, B), move(over_b, A))
        return token

    def project_block(b, after):
        pieces = (own[b], *near[b], *far[b])
        queries[b], kv = project(b, pieces, weights, cosines, sines, flag, after)
        windows.append(share(kv))
        return (kv,)

    def attend_block(b, after):
        held[b], given, token = attend(
            ORDER_IN,
            SCATTER[b],
            scalars,
            queries[b],
            cache,
            q_place,
            k_place,
            tuple(windows[: b + 1]),
            (w_out[0], wo_other),
            after,
        )
        send(b, SCATTER[b], given, 2)
        return token

    def shrink(b, bit, after):
        base = handed[b] if bit == 0 else None
        held[b], given, token = halve(held[b], sent[b], after, base, SCATTER[b])
        send(b, SCATTER[b], given, bit)
        if bit == 0:
            results[b] = jnp.concatenate(
                [
                    (a + r.astype(jnp.float32)).astype(jnp.bfloat16)
                    for a, r in zip(held[b], sent[b])
                ],
                axis=1,
            )
        return token

    t = start_block(0, (cosines, sines, scalars, q_place, k_place, *arrived))
    t = grow(0, (*t, wo_other[:8, :128]))
    t = start_block(1, t)
    t = project_block(0, t)
    t = grow(1, t)
    t = start_block(2, t)
    t = attend_block(0, t)
    t = project_block(1, t)
    t = grow(2, t)
    t = attend_block(1, t)
    t = shrink(0, 1, t)
    t = project_block(2, t)
    t = shrink(1, 1, t)
    t = shrink(0, 0, t)
    t = attend_block(2, t)
    t = shrink(1, 0, t)
    t = shrink(2, 1, t)
    t = shrink(2, 0, t)
    return jnp.stack(results)[None]


def solution(mesh):
    placed = (
        P("section", None, "tensor", None),
        P("section", None),
        P("section", None, "tensor"),
        P("section", None, None, "tensor"),
        P("section", "tensor", None),
        P("section", None, None, None),
        P("section", None),
    )
    return jax.shard_map(
        shards,
        mesh=mesh,
        in_specs=placed,
        out_specs=P("section", None, "tensor", None),
        check_vma=False,
    )
```

```python
import functools
import math

import jax
import jax.numpy as jnp
from jax import lax
from jax.experimental import pallas as pl
from jax.experimental.pallas import tpu as pltpu
from jax.sharding import PartitionSpec as P

HD = 128
BLOCK = 384
CACHE = 384
D = 8192
NZ = 4
SHARD = 24
ROWS = 192
K_CHUNK = 1024
N_CHUNK = 2048
PROJECT_COST = (12,0,12)
ATTEND_COST = (0,12,12)
Y, A, B = (1, 0), (0, 1), (0, 3)

HALF = D // 2
PIECE = 2 * SHARD

ORDER_IN = (Y, A, B)
SCATTER = (
    ((0, 8192, (A, B, Y)),),
    ((0, 4096, (B, Y, A)), (4096, 4096, (A, B, Y)),),
    ((0, 4096, (Y, A, B)), (4096, 4096, (A, B, Y)),),
)


def steps_to(order, block):
    y = z = 0
    for bit in range(3):
        if block >> bit & 1:
            y ^= order[bit][0]
            z ^= order[bit][1]
    return y, z


def reorder(source, target):
    known = [steps_to(source, block) for block in range(8)]
    return [known.index(steps_to(target, block)) for block in range(8)]


def tensor_index(y, z, c):
    return (y * NZ + z) * 2 + c


def move(value, step=(0, 0), dc=0):
    pairs = []
    for y in range(2):
        for z in range(NZ):
            for c in range(2):
                pairs.append((tensor_index(y, z, c), tensor_index(y ^ step[0], z ^ step[1], c ^ dc)))
    return lax.ppermute(value, "tensor", pairs)


def from_behind(value, dy=0):
    sections = lax.axis_size("section")
    tensors = 4 * NZ
    pairs = []
    for s in range(sections):
        for t in range(tensors):
            target = (s + 1) % sections * tensors + (t ^ dy * 2 * NZ)
            pairs.append((s * tensors + t, target))
    return lax.ppermute(value, ("section", "tensor"), pairs)


ANY = pl.BlockSpec(memory_space=pl.ANY)
HBM = pl.BlockSpec(memory_space=pltpu.HBM)


def params(mib):
    return pltpu.CompilerParams(vmem_limit_bytes=mib * 2**20)


def cost(giga=0):
    return pl.CostEstimate(flops=giga * 10**9, bytes_accessed=0, transcendentals=0)


def bf16(*shape):
    return jax.ShapeDtypeStruct(shape, jnp.bfloat16)


def f32(*shape):
    return jax.ShapeDtypeStruct(shape, jnp.float32)


def wide(ref):
    return ref[...].astype(jnp.float32)


def full_spec(shape):
    return pl.BlockSpec(shape, lambda i, n=len(shape): (0,) * n)


def small(kernel, ins, outs, after, name, mib=16):
    picked = [isinstance(a, tuple) for a in ins]
    specs = [
        pl.BlockSpec((None, SHARD, D), lambda i, which=a[1]: (which, 0, 0))
        if is_picked
        else full_spec(a.shape)
        for a, is_picked in zip(ins, picked)
    ]
    ins = [a[0] if is_picked else a for a, is_picked in zip(ins, picked)]

    def body(*refs):
        kernel(refs[: len(ins)], refs[len(ins) + len(after) : -1])
        refs[-1][...] = jnp.zeros((8, 128), jnp.float32)

    outs = list(outs) + [f32(8, 128)]
    *results, token = pl.pallas_call(
        body,
        grid=(1,),
        in_specs=specs + [ANY] * len(after),
        out_specs=[full_spec(o.shape) for o in outs],
        out_shape=outs,
        compiler_params=params(mib),
        cost_estimate=cost(),
        name=name,
    )(*ins, *after)
    return results, (token,)


def norm(mine, other, gain, after):
    def kernel(ins, outs):
        rows = jnp.concatenate([wide(ins[0]), wide(ins[1])], axis=0)
        mean = jnp.mean(rows * rows, axis=1, keepdims=True)
        outs[0][...] = (rows * lax.rsqrt(mean + 1e-05) * wide(ins[2])).astype(jnp.bfloat16)

    return small(kernel, (mine, other, gain), [bf16(PIECE, D)], after, "norm")


def parts(over_a, over_b, after):
    def kernel(ins, outs):
        outs[0][...] = ins[0][:, :HALF]
        outs[1][...] = ins[1][:, HALF:]

    return small(kernel, (over_a, over_b), [bf16(PIECE, HALF)] * 2, after, "parts")


def halve(kept, received, after, base=None, lanes=()):
    def kernel(ins, outs):
        for lane in range(len(kept)):
            rows = wide(ins[2 * lane]) + wide(ins[2 * lane + 1])
            half = rows.shape[0] // 2
            keep = rows[:half]
            if base is not None:
                start, width, _ = lanes[lane]
                keep = keep + ins[-1][:, start : start + width].astype(jnp.float32)
            outs[2 * lane][...] = keep
            outs[2 * lane + 1][...] = rows[half:].astype(jnp.bfloat16)

    ins = [a for pair in zip(kept, received) for a in pair]
    if base is not None:
        ins.append(base)
    outs = []
    for a in kept:
        half = (a.shape[0] // 2, a.shape[1])
        outs += [f32(*half), bf16(*half)]
    results, token = small(kernel, ins, outs, after, "halve")
    return results[0::2], results[1::2], token


def project_kernel(
    own, over_a, over_b, far_a, far_b, wq_mine, wq_other, wkv_mine, wkv_other, cosine, sine, flag, *refs
):
    query, kv, acc_q, acc_kv, wq, wkv, sems = refs[-7:]
    step = pl.program_id(0)
    steps = pl.num_programs(0)

    def fetch(k):
        rows = pl.ds(pl.multiple_of(k * K_CHUNK, K_CHUNK), K_CHUNK)
        return [
            pltpu.make_async_copy(source.at[rows], target.at[half, k], sems.at[kind + half, k])
            for half, kind, source, target in (
                (0, 0, wq_mine, wq),
                (1, 0, wq_other, wq),
                (0, 2, wkv_mine, wkv),
                (1, 2, wkv_other, wkv),
            )
        ]

    @pl.when(step == 0)
    def _():
        for k in range(D // K_CHUNK):
            for copy in fetch(k):
                copy.start()

    for copy in fetch(step):
        copy.wait()
    far = jnp.where(step < steps // 2, far_a[...], far_b[...])
    x = jnp.concatenate([own[...], over_a[...], over_b[...], far], axis=0)

    @pl.when(step == 0)
    def _():
        acc_q[...] = jnp.zeros_like(acc_q)
        acc_kv[...] = jnp.zeros_like(acc_kv)

    for half in range(2):
        acc_q[:, half * 512 : half * 512 + 512] += jnp.dot(
            x, wq[half, step], preferred_element_type=jnp.float32
        )
    both = jnp.concatenate([wkv[0, step], wkv[1, step]], axis=1)
    acc_kv[...] += jnp.dot(x, both, preferred_element_type=jnp.float32)

    @pl.when(step == steps - 1)
    def _():
        cos = cosine[...]
        sin = sine[...]

        def turn(u):
            return u * cos + pltpu.roll(u, HD // 2, 1) * sin

        for head in range(8):
            query[head] = turn(acc_q[:, head * HD : head * HD + HD]).astype(jnp.bfloat16)
        first = flag[...] == 0
        mine = acc_kv[:, :HD]
        other = acc_kv[:, HD:]
        low = jnp.where(first, mine, other)
        high = jnp.where(first, other, mine)
        lower = lax.broadcasted_iota(jnp.int32, (ROWS, HD), 1) < HD // 2
        keys = jnp.where(lower, low, pltpu.roll(high, HD // 2, 1))
        values = jnp.where(lower, pltpu.roll(low, HD // 2, 1), high)
        keys = keys.astype(jnp.bfloat16).astype(jnp.float32)
        kv[0] = turn(keys).astype(jnp.bfloat16)
        kv[1] = values.astype(jnp.bfloat16)


def lane_spec(start, width, chunk):
    first = start // chunk
    count = width // chunk
    return pl.BlockSpec(
        (ROWS // 2, chunk), lambda k, *_: (0, jnp.clip(k - first, 0, count - 1))
    )


def project(which, pieces, weights, cosine, sine, flag, after):
    steps = D // K_CHUNK
    near = pl.BlockSpec((PIECE, K_CHUNK), lambda k: (0, k))
    specs = [near, near, near]
    specs.append(pl.BlockSpec((PIECE, K_CHUNK), lambda k: (0, jnp.minimum(k, steps // 2 - 1))))
    specs.append(pl.BlockSpec((PIECE, K_CHUNK), lambda k: (0, jnp.maximum(k - steps // 2, 0))))
    for w in weights:
        specs.append(HBM)
    table = pl.BlockSpec((None, ROWS, HD), lambda k: (which, 0, 0))
    specs += [table, table, full_spec(flag.shape)] + [ANY] * len(after)
    return pl.pallas_call(
        project_kernel,
        out_shape=(bf16(8, ROWS, HD), bf16(2, ROWS, HD)),
        grid=(steps,),
        in_specs=specs,
        out_specs=(
            pl.BlockSpec((8, ROWS, HD), lambda k: (0, 0, 0)),
            pl.BlockSpec((2, ROWS, HD), lambda k: (0, 0, 0)),
        ),
        scratch_shapes=[
            pltpu.VMEM((ROWS, 1024), jnp.float32),
            pltpu.VMEM((ROWS, 2 * HD), jnp.float32),
            pltpu.VMEM((2, steps, K_CHUNK, 512), jnp.bfloat16),
            pltpu.VMEM((2, steps, K_CHUNK, HD), jnp.bfloat16),
            pltpu.SemaphoreType.DMA((4, steps)),
        ],
        compiler_params=params(44),
        cost_estimate=cost(PROJECT_COST[which]),
        name="project",
    )(*pieces, *weights, cosine, sine, flag, *after)


def attend_kernel(blocks, order, lanes, scalars, query, cache, q_place, k_place, *refs):
    windows = refs[:blocks]
    weights = refs[blocks : blocks + 2]
    count = 2 * len(lanes)
    outs = refs[-5 - count : -5]
    token, raw, attended, wo, sems = refs[-5:]
    step = pl.program_id(0)

    def fetch(n, half):
        return pltpu.make_async_copy(
            weights[half].at[:, pl.ds(pl.multiple_of(n * N_CHUNK, N_CHUNK), N_CHUNK)],
            wo.at[n, pl.ds(half * 512, 512), :],
            sems.at[n, half],
        )

    @pl.when(step == 0)
    def _():
        for n in range(D // N_CHUNK):
            fetch(n, 0).start()
            fetch(n, 1).start()
        token[...] = jnp.zeros((8, 128), jnp.float32)
        scale = math.log2(math.e) / math.sqrt(HD)
        slot = lax.broadcasted_iota(jnp.int32, (1, CACHE), 1)
        cache_bias = jnp.where(slot < scalars[1], 0.0, -1e30)
        causal_bias = jnp.where(k_place[...] <= q_place[...], 0.0, -1e30)
        keys = jnp.concatenate([cache[0]] + [w[c, 0] for w in windows for c in range(2)], axis=0)
        values = jnp.concatenate([cache[1]] + [w[c, 1] for w in windows for c in range(2)], axis=0)
        before = CACHE + (blocks - 1) * BLOCK
        for head in range(8):
            scores = lax.dot_general(
                query[head], keys, (((1,), (1,)), ((), ())), preferred_element_type=jnp.float32
            )
            parts = [scores[:, :CACHE] + cache_bias]
            if blocks > 1:
                parts.append(scores[:, CACHE:before])
            parts.append(scores[:, before:] + causal_bias)
            scores = jnp.concatenate(parts, axis=1)
            top = jnp.max(scores, axis=1, keepdims=True)
            grown = jnp.exp2((scores - top) * scale)
            total = jnp.sum(grown, axis=1, keepdims=True)
            out = jnp.dot(grown.astype(jnp.bfloat16), values, preferred_element_type=jnp.float32)
            raw[:, head * HD : head * HD + HD] = out / total
        for lane, (_, _, target) in enumerate(lanes):
            places = reorder(order, target)
            rows = [raw[p * SHARD : p * SHARD + SHARD] for p in places]
            attended[lane] = jnp.concatenate(rows, axis=0).astype(jnp.bfloat16)

    fetch(step, 0).wait()
    fetch(step, 1).wait()
    for lane, (start, width, _) in enumerate(lanes):
        first, last = start // N_CHUNK, (start + width) // N_CHUNK - 1

        @pl.when(jnp.logical_and(step >= first, step <= last))
        def _(lane=lane):
            term = jnp.dot(attended[lane], wo[step], preferred_element_type=jnp.float32)
            term = term.astype(jnp.bfloat16)
            outs[2 * lane][...] = term[: ROWS // 2]
            outs[2 * lane + 1][...] = term[ROWS // 2 :]


def attend(order, lanes, scalars, query, cache, q_place, k_place, windows, wo, after):
    steps = D // N_CHUNK
    blocks = len(windows)
    whole = lambda a: pl.BlockSpec(a.shape, lambda n, s: (0,) * a.ndim)
    specs = [
        whole(query),
        pl.BlockSpec((2, CACHE, HD), lambda n, s: (0, 0, s[0])),
        whole(q_place),
        whole(k_place),
        *[whole(w) for w in windows],
        HBM,
        HBM,
        *[ANY] * len(after),
    ]
    out_shape = []
    out_specs = []
    for start, width, _ in lanes:
        out_shape += [bf16(ROWS // 2, width)] * 2
        out_specs += [lane_spec(start, width, N_CHUNK)] * 2
    *results, token = pl.pallas_call(
        functools.partial(attend_kernel, blocks, order, lanes),
        out_shape=(*out_shape, f32(8, 128)),
        grid_spec=pltpu.PrefetchScalarGridSpec(
            num_scalar_prefetch=1,
            grid=(steps,),
            in_specs=specs,
            out_specs=(*out_specs, pl.BlockSpec((8, 128), lambda n, s: (0, 0))),
            scratch_shapes=[
                pltpu.VMEM((ROWS, 1024), jnp.float32),
                pltpu.VMEM((len(lanes), ROWS, 1024), jnp.bfloat16),
                pltpu.VMEM((steps, 1024, N_CHUNK), jnp.bfloat16),
                pltpu.SemaphoreType.DMA((steps, 2)),
            ],
        ),
        compiler_params=params(48),
        cost_estimate=cost(ATTEND_COST[blocks - 1]),
        name="attend",
    )(scalars, query, cache, q_place, k_place, *windows, *wo, *after)
    return results[0::2], results[1::2], (token,)


def shards(incoming, norm_gain, w_query, w_key_value, w_out, kv_cache, offsets):
    index = lax.axis_index("tensor")
    core = index % 2
    z = index // 2 % NZ
    y = index // (2 * NZ)
    head = index // 2
    offset = offsets[0, 0]
    handed = []
    beside = []
    for b in range(3):
        handed.append((from_behind(incoming[0, b : b + 1]), 0))
        beside.append((from_behind(incoming[0, b : b + 1], 1), 0))
    pairs = [[i, i + 1] for i in range(0, 4 * NZ, 2)]
    share = lambda a: lax.all_gather(a, "tensor", axis_index_groups=pairs)
    wkv = w_key_value[0].reshape(D, 2 * w_key_value.shape[3])
    wq_other = move(w_query[0], dc=1)
    wkv_other = move(wkv, dc=1)
    wo_other = move(w_out[0], dc=1)
    weights = (w_query[0], wq_other, wkv, wkv_other)
    arrived = (wq_other[:8, :128], wkv_other[:8, :128])
    flag = jnp.full((1, HD), core, jnp.int32)

    within = jnp.arange(SHARD, dtype=jnp.int32)
    freq = 500000.0 ** (-jnp.arange(HD // 2, dtype=jnp.float32) * 2.0 / HD)
    def places(c):
        moves = [steps_to(ORDER_IN, block) for block in range(8)]
        return jnp.concatenate(
            [tensor_index(y ^ dy, z ^ dz, c) * SHARD + within for dy, dz in moves]
        )

    mine = places(core)
    q_place = mine[:, None]
    k_place = jnp.concatenate([places(0), places(1)])[None, :]
    position = (offsets[0][:, None] + mine[None, :]).astype(jnp.float32)
    angle = position[:, :, None] * freq
    cos = jnp.cos(angle)
    sin = jnp.sin(angle)
    cosines = jnp.concatenate([cos, cos], axis=2)
    sines = jnp.concatenate([-sin, sin], axis=2)
    scalars = jnp.stack([head, offset])
    cache = kv_cache[0]

    held = [None] * 3
    sent = [None] * 3
    queries = [None] * 3
    windows = []
    results = [None] * 3

    def send(b, lanes, values, bit):
        sent[b] = [move(a, lane[2][bit]) for a, lane in zip(values, lanes)]

    own = [None] * 3
    near = [None] * 3
    far = [None] * 3

    def start_block(b, after):
        (own[b],), token = norm(handed[b], beside[b], norm_gain, after)
        near[b] = (move(own[b], A), move(own[b], B))
        return token

    def grow(b, after):
        (over_a, over_b), token = parts(*near[b], after)
        far[b] = (move(over_a, B), move(over_b, A))
        return token

    def project_block(b, after):
        pieces = (own[b], *near[b], *far[b])
        queries[b], kv = project(b, pieces, weights, cosines, sines, flag, after)
        windows.append(share(kv))
        return (kv,)

    def attend_block(b, after):
        held[b], given, token = attend(
            ORDER_IN,
            SCATTER[b],
            scalars,
            queries[b],
            cache,
            q_place,
            k_place,
            tuple(windows[: b + 1]),
            (w_out[0], wo_other),
            after,
        )
        send(b, SCATTER[b], given, 2)
        return token

    def shrink(b, bit, after):
        base = handed[b] if bit == 0 else None
        held[b], given, token = halve(held[b], sent[b], after, base, SCATTER[b])
        send(b, SCATTER[b], given, bit)
        if bit == 0:
            results[b] = jnp.concatenate(
                [
                    (a + r.astype(jnp.float32)).astype(jnp.bfloat16)
                    for a, r in zip(held[b], sent[b])
                ],
                axis=1,
            )
        return token

    t = start_block(0, (cosines, sines, scalars, q_place, k_place, *arrived))
    t = grow(0, (*t, wo_other[:8, :128]))
    t = start_block(1, t)
    t = project_block(0, t)
    t = grow(1, t)
    t = start_block(2, t)
    t = attend_block(0, t)
    t = project_block(1, t)
    t = grow(2, t)
    t = attend_block(1, t)
    t = shrink(0, 1, t)
    t = project_block(2, t)
    t = shrink(1, 1, t)
    t = shrink(0, 0, t)
    t = attend_block(2, t)
    t = shrink(1, 0, t)
    t = shrink(2, 1, t)
    t = shrink(2, 0, t)
    return jnp.stack(results)[None]


def solution(mesh):
    placed = (
        P("section", None, "tensor", None),
        P("section", None),
        P("section", None, "tensor"),
        P("section", None, None, "tensor"),
        P("section", "tensor", None),
        P("section", None, None, None),
        P("section", None),
    )
    return jax.shard_map(
        shards,
        mesh=mesh,
        in_specs=placed,
        out_specs=P("section", None, "tensor", None),
        check_vma=False,
    )
```

```python
import functools
import math

import jax
import jax.numpy as jnp
from jax import lax
from jax.experimental import pallas as pl
from jax.experimental.pallas import tpu as pltpu
from jax.sharding import PartitionSpec as P

HD = 128
BLOCK = 384
CACHE = 384
D = 8192
NZ = 4
SHARD = 24
ROWS = 192
K_CHUNK = 1024
N_CHUNK = 2048
PROJECT_COST = (12,12,12)
ATTEND_COST = (0,12,12)
Y, A, B = (1, 0), (0, 1), (0, 3)

HALF = D // 2
PIECE = 2 * SHARD

ORDER_IN = (Y, A, B)
SCATTER = (
    ((0, 8192, (A, B, Y)),),
    ((0, 4096, (B, Y, A)), (4096, 4096, (A, B, Y)),),
    ((0, 4096, (Y, A, B)), (4096, 4096, (A, B, Y)),),
)


def steps_to(order, block):
    y = z = 0
    for bit in range(3):
        if block >> bit & 1:
            y ^= order[bit][0]
            z ^= order[bit][1]
    return y, z


def reorder(source, target):
    known = [steps_to(source, block) for block in range(8)]
    return [known.index(steps_to(target, block)) for block in range(8)]


def tensor_index(y, z, c):
    return (y * NZ + z) * 2 + c


def move(value, step=(0, 0), dc=0):
    pairs = []
    for y in range(2):
        for z in range(NZ):
            for c in range(2):
                pairs.append((tensor_index(y, z, c), tensor_index(y ^ step[0], z ^ step[1], c ^ dc)))
    return lax.ppermute(value, "tensor", pairs)


def from_behind(value, dy=0):
    sections = lax.axis_size("section")
    tensors = 4 * NZ
    pairs = []
    for s in range(sections):
        for t in range(tensors):
            target = (s + 1) % sections * tensors + (t ^ dy * 2 * NZ)
            pairs.append((s * tensors + t, target))
    return lax.ppermute(value, ("section", "tensor"), pairs)


ANY = pl.BlockSpec(memory_space=pl.ANY)
HBM = pl.BlockSpec(memory_space=pltpu.HBM)


def params(mib):
    return pltpu.CompilerParams(vmem_limit_bytes=mib * 2**20)


def cost(giga=0):
    return pl.CostEstimate(flops=giga * 10**9, bytes_accessed=0, transcendentals=0)


def bf16(*shape):
    return jax.ShapeDtypeStruct(shape, jnp.bfloat16)


def f32(*shape):
    return jax.ShapeDtypeStruct(shape, jnp.float32)


def wide(ref):
    return ref[...].astype(jnp.float32)


def full_spec(shape):
    return pl.BlockSpec(shape, lambda i, n=len(shape): (0,) * n)


def small(kernel, ins, outs, after, name, mib=16):
    picked = [isinstance(a, tuple) for a in ins]
    specs = [
        pl.BlockSpec((None, SHARD, D), lambda i, which=a[1]: (which, 0, 0))
        if is_picked
        else full_spec(a.shape)
        for a, is_picked in zip(ins, picked)
    ]
    ins = [a[0] if is_picked else a for a, is_picked in zip(ins, picked)]

    def body(*refs):
        kernel(refs[: len(ins)], refs[len(ins) + len(after) : -1])
        refs[-1][...] = jnp.zeros((8, 128), jnp.float32)

    outs = list(outs) + [f32(8, 128)]
    *results, token = pl.pallas_call(
        body,
        grid=(1,),
        in_specs=specs + [ANY] * len(after),
        out_specs=[full_spec(o.shape) for o in outs],
        out_shape=outs,
        compiler_params=params(mib),
        cost_estimate=cost(),
        name=name,
    )(*ins, *after)
    return results, (token,)


def norm(mine, other, gain, after):
    def kernel(ins, outs):
        rows = jnp.concatenate([wide(ins[0]), wide(ins[1])], axis=0)
        mean = jnp.mean(rows * rows, axis=1, keepdims=True)
        outs[0][...] = (rows * lax.rsqrt(mean + 1e-05) * wide(ins[2])).astype(jnp.bfloat16)

    return small(kernel, (mine, other, gain), [bf16(PIECE, D)], after, "norm")


def parts(over_a, over_b, after):
    def kernel(ins, outs):
        outs[0][...] = ins[0][:, :HALF]
        outs[1][...] = ins[1][:, HALF:]

    return small(kernel, (over_a, over_b), [bf16(PIECE, HALF)] * 2, after, "parts")


def halve(kept, received, after, base=None, lanes=()):
    def kernel(ins, outs):
        for lane in range(len(kept)):
            rows = wide(ins[2 * lane]) + wide(ins[2 * lane + 1])
            half = rows.shape[0] // 2
            keep = rows[:half]
            if base is not None:
                start, width, _ = lanes[lane]
                keep = keep + ins[-1][:, start : start + width].astype(jnp.float32)
            outs[2 * lane][...] = keep
            outs[2 * lane + 1][...] = rows[half:].astype(jnp.bfloat16)

    ins = [a for pair in zip(kept, received) for a in pair]
    if base is not None:
        ins.append(base)
    outs = []
    for a in kept:
        half = (a.shape[0] // 2, a.shape[1])
        outs += [f32(*half), bf16(*half)]
    results, token = small(kernel, ins, outs, after, "halve")
    return results[0::2], results[1::2], token


def project_kernel(
    own, over_a, over_b, far_a, far_b, wq_mine, wq_other, wkv_mine, wkv_other, cosine, sine, flag, *refs
):
    query, kv, acc_q, acc_kv, wq, wkv, sems = refs[-7:]
    step = pl.program_id(0)
    steps = pl.num_programs(0)

    def fetch(k):
        rows = pl.ds(pl.multiple_of(k * K_CHUNK, K_CHUNK), K_CHUNK)
        return [
            pltpu.make_async_copy(source.at[rows], target.at[half, k], sems.at[kind + half, k])
            for half, kind, source, target in (
                (0, 0, wq_mine, wq),
                (1, 0, wq_other, wq),
                (0, 2, wkv_mine, wkv),
                (1, 2, wkv_other, wkv),
            )
        ]

    @pl.when(step == 0)
    def _():
        for k in range(D // K_CHUNK):
            for copy in fetch(k):
                copy.start()

    for copy in fetch(step):
        copy.wait()
    far = jnp.where(step < steps // 2, far_a[...], far_b[...])
    x = jnp.concatenate([own[...], over_a[...], over_b[...], far], axis=0)

    @pl.when(step == 0)
    def _():
        acc_q[...] = jnp.zeros_like(acc_q)
        acc_kv[...] = jnp.zeros_like(acc_kv)

    for half in range(2):
        acc_q[:, half * 512 : half * 512 + 512] += jnp.dot(
            x, wq[half, step], preferred_element_type=jnp.float32
        )
    both = jnp.concatenate([wkv[0, step], wkv[1, step]], axis=1)
    acc_kv[...] += jnp.dot(x, both, preferred_element_type=jnp.float32)

    @pl.when(step == steps - 1)
    def _():
        cos = cosine[...]
        sin = sine[...]

        def turn(u):
            return u * cos + pltpu.roll(u, HD // 2, 1) * sin

        for head in range(8):
            query[head] = turn(acc_q[:, head * HD : head * HD + HD]).astype(jnp.bfloat16)
        first = flag[...] == 0
        mine = acc_kv[:, :HD]
        other = acc_kv[:, HD:]
        low = jnp.where(first, mine, other)
        high = jnp.where(first, other, mine)
        lower = lax.broadcasted_iota(jnp.int32, (ROWS, HD), 1) < HD // 2
        keys = jnp.where(lower, low, pltpu.roll(high, HD // 2, 1))
        values = jnp.where(lower, pltpu.roll(low, HD // 2, 1), high)
        keys = keys.astype(jnp.bfloat16).astype(jnp.float32)
        kv[0] = turn(keys).astype(jnp.bfloat16)
        kv[1] = values.astype(jnp.bfloat16)


def lane_spec(start, width, chunk):
    first = start // chunk
    count = width // chunk
    return pl.BlockSpec(
        (ROWS // 2, chunk), lambda k, *_: (0, jnp.clip(k - first, 0, count - 1))
    )


def project(which, pieces, weights, cosine, sine, flag, after):
    steps = D // K_CHUNK
    near = pl.BlockSpec((PIECE, K_CHUNK), lambda k: (0, k))
    specs = [near, near, near]
    specs.append(pl.BlockSpec((PIECE, K_CHUNK), lambda k: (0, jnp.minimum(k, steps // 2 - 1))))
    specs.append(pl.BlockSpec((PIECE, K_CHUNK), lambda k: (0, jnp.maximum(k - steps // 2, 0))))
    for w in weights:
        specs.append(HBM)
    table = pl.BlockSpec((None, ROWS, HD), lambda k: (which, 0, 0))
    specs += [table, table, full_spec(flag.shape)] + [ANY] * len(after)
    return pl.pallas_call(
        project_kernel,
        out_shape=(bf16(8, ROWS, HD), bf16(2, ROWS, HD)),
        grid=(steps,),
        in_specs=specs,
        out_specs=(
            pl.BlockSpec((8, ROWS, HD), lambda k: (0, 0, 0)),
            pl.BlockSpec((2, ROWS, HD), lambda k: (0, 0, 0)),
        ),
        scratch_shapes=[
            pltpu.VMEM((ROWS, 1024), jnp.float32),
            pltpu.VMEM((ROWS, 2 * HD), jnp.float32),
            pltpu.VMEM((2, steps, K_CHUNK, 512), jnp.bfloat16),
            pltpu.VMEM((2, steps, K_CHUNK, HD), jnp.bfloat16),
            pltpu.SemaphoreType.DMA((4, steps)),
        ],
        compiler_params=params(52),
        cost_estimate=cost(PROJECT_COST[which]),
        name="project",
    )(*pieces, *weights, cosine, sine, flag, *after)


def attend_kernel(blocks, order, lanes, scalars, query, cache, q_place, k_place, *refs):
    windows = refs[:blocks]
    weights = refs[blocks : blocks + 2]
    count = 2 * len(lanes)
    outs = refs[-5 - count : -5]
    token, raw, attended, wo, sems = refs[-5:]
    step = pl.program_id(0)

    def fetch(n, half):
        return pltpu.make_async_copy(
            weights[half].at[:, pl.ds(pl.multiple_of(n * N_CHUNK, N_CHUNK), N_CHUNK)],
            wo.at[n, pl.ds(half * 512, 512), :],
            sems.at[n, half],
        )

    @pl.when(step == 0)
    def _():
        for n in range(D // N_CHUNK):
            fetch(n, 0).start()
            fetch(n, 1).start()
        token[...] = jnp.zeros((8, 128), jnp.float32)
        scale = math.log2(math.e) / math.sqrt(HD)
        slot = lax.broadcasted_iota(jnp.int32, (1, CACHE), 1)
        cache_bias = jnp.where(slot < scalars[1], 0.0, -1e30)
        causal_bias = jnp.where(k_place[...] <= q_place[...], 0.0, -1e30)
        keys = jnp.concatenate([cache[0]] + [w[c, 0] for w in windows for c in range(2)], axis=0)
        values = jnp.concatenate([cache[1]] + [w[c, 1] for w in windows for c in range(2)], axis=0)
        before = CACHE + (blocks - 1) * BLOCK
        for head in range(8):
            scores = lax.dot_general(
                query[head], keys, (((1,), (1,)), ((), ())), preferred_element_type=jnp.float32
            )
            parts = [scores[:, :CACHE] + cache_bias]
            if blocks > 1:
                parts.append(scores[:, CACHE:before])
            parts.append(scores[:, before:] + causal_bias)
            scores = jnp.concatenate(parts, axis=1)
            top = jnp.max(scores, axis=1, keepdims=True)
            grown = jnp.exp2((scores - top) * scale)
            total = jnp.sum(grown, axis=1, keepdims=True)
            out = jnp.dot(grown.astype(jnp.bfloat16), values, preferred_element_type=jnp.float32)
            raw[:, head * HD : head * HD + HD] = out / total
        for lane, (_, _, target) in enumerate(lanes):
            places = reorder(order, target)
            rows = [raw[p * SHARD : p * SHARD + SHARD] for p in places]
            attended[lane] = jnp.concatenate(rows, axis=0).astype(jnp.bfloat16)

    fetch(step, 0).wait()
    fetch(step, 1).wait()
    for lane, (start, width, _) in enumerate(lanes):
        first, last = start // N_CHUNK, (start + width) // N_CHUNK - 1

        @pl.when(jnp.logical_and(step >= first, step <= last))
        def _(lane=lane):
            term = jnp.dot(attended[lane], wo[step], preferred_element_type=jnp.float32)
            term = term.astype(jnp.bfloat16)
            outs[2 * lane][...] = term[: ROWS // 2]
            outs[2 * lane + 1][...] = term[ROWS // 2 :]


def attend(order, lanes, scalars, query, cache, q_place, k_place, windows, wo, after):
    steps = D // N_CHUNK
    blocks = len(windows)
    whole = lambda a: pl.BlockSpec(a.shape, lambda n, s: (0,) * a.ndim)
    specs = [
        whole(query),
        pl.BlockSpec((2, CACHE, HD), lambda n, s: (0, 0, s[0])),
        whole(q_place),
        whole(k_place),
        *[whole(w) for w in windows],
        HBM,
        HBM,
        *[ANY] * len(after),
    ]
    out_shape = []
    out_specs = []
    for start, width, _ in lanes:
        out_shape += [bf16(ROWS // 2, width)] * 2
        out_specs += [lane_spec(start, width, N_CHUNK)] * 2
    *results, token = pl.pallas_call(
        functools.partial(attend_kernel, blocks, order, lanes),
        out_shape=(*out_shape, f32(8, 128)),
        grid_spec=pltpu.PrefetchScalarGridSpec(
            num_scalar_prefetch=1,
            grid=(steps,),
            in_specs=specs,
            out_specs=(*out_specs, pl.BlockSpec((8, 128), lambda n, s: (0, 0))),
            scratch_shapes=[
                pltpu.VMEM((ROWS, 1024), jnp.float32),
                pltpu.VMEM((len(lanes), ROWS, 1024), jnp.bfloat16),
                pltpu.VMEM((steps, 1024, N_CHUNK), jnp.bfloat16),
                pltpu.SemaphoreType.DMA((steps, 2)),
            ],
        ),
        compiler_params=params(52),
        cost_estimate=cost(ATTEND_COST[blocks - 1]),
        name="attend",
    )(scalars, query, cache, q_place, k_place, *windows, *wo, *after)
    return results[0::2], results[1::2], (token,)


def shards(incoming, norm_gain, w_query, w_key_value, w_out, kv_cache, offsets):
    index = lax.axis_index("tensor")
    core = index % 2
    z = index // 2 % NZ
    y = index // (2 * NZ)
    head = index // 2
    offset = offsets[0, 0]
    handed = []
    beside = []
    for b in range(3):
        handed.append((from_behind(incoming[0, b : b + 1]), 0))
        beside.append((from_behind(incoming[0, b : b + 1], 1), 0))
    pairs = [[i, i + 1] for i in range(0, 4 * NZ, 2)]
    share = lambda a: lax.all_gather(a, "tensor", axis_index_groups=pairs)
    wkv = w_key_value[0].reshape(D, 2 * w_key_value.shape[3])
    wq_other = move(w_query[0], dc=1)
    wkv_other = move(wkv, dc=1)
    wo_other = move(w_out[0], dc=1)
    weights = (w_query[0], wq_other, wkv, wkv_other)
    arrived = (wq_other[:8, :128], wkv_other[:8, :128])
    flag = jnp.full((1, HD), core, jnp.int32)

    within = jnp.arange(SHARD, dtype=jnp.int32)
    freq = 500000.0 ** (-jnp.arange(HD // 2, dtype=jnp.float32) * 2.0 / HD)
    def places(c):
        moves = [steps_to(ORDER_IN, block) for block in range(8)]
        return jnp.concatenate(
            [tensor_index(y ^ dy, z ^ dz, c) * SHARD + within for dy, dz in moves]
        )

    mine = places(core)
    q_place = mine[:, None]
    k_place = jnp.concatenate([places(0), places(1)])[None, :]
    position = (offsets[0][:, None] + mine[None, :]).astype(jnp.float32)
    angle = position[:, :, None] * freq
    cos = jnp.cos(angle)
    sin = jnp.sin(angle)
    cosines = jnp.concatenate([cos, cos], axis=2)
    sines = jnp.concatenate([-sin, sin], axis=2)
    scalars = jnp.stack([head, offset])
    cache = kv_cache[0]

    held = [None] * 3
    sent = [None] * 3
    queries = [None] * 3
    windows = []
    results = [None] * 3

    def send(b, lanes, values, bit):
        sent[b] = [move(a, lane[2][bit]) for a, lane in zip(values, lanes)]

    own = [None] * 3
    near = [None] * 3
    far = [None] * 3

    def start_block(b, after):
        (own[b],), token = norm(handed[b], beside[b], norm_gain, after)
        near[b] = (move(own[b], A), move(own[b], B))
        return token

    def grow(b, after):
        (over_a, over_b), token = parts(*near[b], after)
        far[b] = (move(over_a, B), move(over_b, A))
        return token

    def project_block(b, after):
        pieces = (own[b], *near[b], *far[b])
        queries[b], kv = project(b, pieces, weights, cosines, sines, flag, after)
        windows.append(share(kv))
        return (kv,)

    def attend_block(b, after):
        held[b], given, token = attend(
            ORDER_IN,
            SCATTER[b],
            scalars,
            queries[b],
            cache,
            q_place,
            k_place,
            tuple(windows[: b + 1]),
            (w_out[0], wo_other),
            after,
        )
        send(b, SCATTER[b], given, 2)
        return token

    def shrink(b, bit, after):
        base = handed[b] if bit == 0 else None
        held[b], given, token = halve(held[b], sent[b], after, base, SCATTER[b])
        send(b, SCATTER[b], given, bit)
        if bit == 0:
            results[b] = jnp.concatenate(
                [
                    (a + r.astype(jnp.float32)).astype(jnp.bfloat16)
                    for a, r in zip(held[b], sent[b])
                ],
                axis=1,
            )
        return token

    t = start_block(0, (cosines, sines, scalars, q_place, k_place, *arrived))
    t = grow(0, (*t, wo_other[:8, :128]))
    t = start_block(1, t)
    t = project_block(0, t)
    t = grow(1, t)
    t = start_block(2, t)
    t = attend_block(0, t)
    t = project_block(1, t)
    t = grow(2, t)
    t = attend_block(1, t)
    t = shrink(0, 1, t)
    t = project_block(2, t)
    t = shrink(1, 1, t)
    t = shrink(0, 0, t)
    t = attend_block(2, t)
    t = shrink(1, 0, t)
    t = shrink(2, 1, t)
    t = shrink(2, 0, t)
    return jnp.stack(results)[None]


def solution(mesh):
    placed = (
        P("section", None, "tensor", None),
        P("section", None),
        P("section", None, "tensor"),
        P("section", None, None, "tensor"),
        P("section", "tensor", None),
        P("section", None, None, None),
        P("section", None),
    )
    return jax.shard_map(
        shards,
        mesh=mesh,
        in_specs=placed,
        out_specs=P("section", None, "tensor", None),
        check_vma=False,
    )
```

```python
import functools
import math

import jax
import jax.numpy as jnp
from jax import lax
from jax.experimental import pallas as pl
from jax.experimental.pallas import tpu as pltpu
from jax.sharding import PartitionSpec as P

HD = 128
BLOCK = 384
CACHE = 384
D = 8192
NZ = 4
SHARD = 24
ROWS = 192
K_CHUNK = 1024
AHEAD = 2
N_CHUNK = 2048
PROJECT_COST = (12,12,12)
ATTEND_COST = (0,12,12)
Y, A, B = (1, 0), (0, 1), (0, 3)

HALF = D // 2
PIECE = 2 * SHARD

ORDER_IN = (Y, A, B)
SCATTER = (
    ((0, 8192, (A, B, Y)),),
    ((0, 4096, (B, Y, A)), (4096, 4096, (A, B, Y)),),
    ((0, 4096, (Y, A, B)), (4096, 4096, (A, B, Y)),),
)


def steps_to(order, block):
    y = z = 0
    for bit in range(3):
        if block >> bit & 1:
            y ^= order[bit][0]
            z ^= order[bit][1]
    return y, z


def reorder(source, target):
    known = [steps_to(source, block) for block in range(8)]
    return [known.index(steps_to(target, block)) for block in range(8)]


def tensor_index(y, z, c):
    return (y * NZ + z) * 2 + c


def move(value, step=(0, 0), dc=0):
    pairs = []
    for y in range(2):
        for z in range(NZ):
            for c in range(2):
                pairs.append((tensor_index(y, z, c), tensor_index(y ^ step[0], z ^ step[1], c ^ dc)))
    return lax.ppermute(value, "tensor", pairs)


def from_behind(value, dy=0):
    sections = lax.axis_size("section")
    tensors = 4 * NZ
    pairs = []
    for s in range(sections):
        for t in range(tensors):
            target = (s + 1) % sections * tensors + (t ^ dy * 2 * NZ)
            pairs.append((s * tensors + t, target))
    return lax.ppermute(value, ("section", "tensor"), pairs)


ANY = pl.BlockSpec(memory_space=pl.ANY)
HBM = pl.BlockSpec(memory_space=pltpu.HBM)


def params(mib):
    return pltpu.CompilerParams(vmem_limit_bytes=mib * 2**20)


def cost(giga=0):
    return pl.CostEstimate(flops=giga * 10**9, bytes_accessed=0, transcendentals=0)


def bf16(*shape):
    return jax.ShapeDtypeStruct(shape, jnp.bfloat16)


def f32(*shape):
    return jax.ShapeDtypeStruct(shape, jnp.float32)


def wide(ref):
    return ref[...].astype(jnp.float32)


def full_spec(shape):
    return pl.BlockSpec(shape, lambda i, n=len(shape): (0,) * n)


def small(kernel, ins, outs, after, name, mib=16):
    picked = [isinstance(a, tuple) for a in ins]
    specs = [
        pl.BlockSpec((None, SHARD, D), lambda i, which=a[1]: (which, 0, 0))
        if is_picked
        else full_spec(a.shape)
        for a, is_picked in zip(ins, picked)
    ]
    ins = [a[0] if is_picked else a for a, is_picked in zip(ins, picked)]

    def body(*refs):
        kernel(refs[: len(ins)], refs[len(ins) + len(after) : -1])
        refs[-1][...] = jnp.zeros((8, 128), jnp.float32)

    outs = list(outs) + [f32(8, 128)]
    *results, token = pl.pallas_call(
        body,
        grid=(1,),
        in_specs=specs + [ANY] * len(after),
        out_specs=[full_spec(o.shape) for o in outs],
        out_shape=outs,
        compiler_params=params(mib),
        cost_estimate=cost(),
        name=name,
    )(*ins, *after)
    return results, (token,)


def norm(mine, other, gain, after):
    def kernel(ins, outs):
        rows = jnp.concatenate([wide(ins[0]), wide(ins[1])], axis=0)
        mean = jnp.mean(rows * rows, axis=1, keepdims=True)
        outs[0][...] = (rows * lax.rsqrt(mean + 1e-05) * wide(ins[2])).astype(jnp.bfloat16)

    return small(kernel, (mine, other, gain), [bf16(PIECE, D)], after, "norm")


def parts(over_a, over_b, after):
    def kernel(ins, outs):
        outs[0][...] = ins[0][:, :HALF]
        outs[1][...] = ins[1][:, HALF:]

    return small(kernel, (over_a, over_b), [bf16(PIECE, HALF)] * 2, after, "parts")


def halve(kept, received, after, base=None, lanes=()):
    def kernel(ins, outs):
        for lane in range(len(kept)):
            rows = wide(ins[2 * lane]) + wide(ins[2 * lane + 1])
            half = rows.shape[0] // 2
            keep = rows[:half]
            if base is not None:
                start, width, _ = lanes[lane]
                keep = keep + ins[-1][:, start : start + width].astype(jnp.float32)
            outs[2 * lane][...] = keep
            outs[2 * lane + 1][...] = rows[half:].astype(jnp.bfloat16)

    ins = [a for pair in zip(kept, received) for a in pair]
    if base is not None:
        ins.append(base)
    outs = []
    for a in kept:
        half = (a.shape[0] // 2, a.shape[1])
        outs += [f32(*half), bf16(*half)]
    results, token = small(kernel, ins, outs, after, "halve")
    return results[0::2], results[1::2], token


def project_kernel(
    own, over_a, over_b, far_a, far_b, wq_mine, wq_other, wkv_mine, wkv_other, cosine, sine, flag, *refs
):
    query, kv, acc_q, acc_kv, wq, wkv, sems = refs[-7:]
    step = pl.program_id(0)
    steps = pl.num_programs(0)

    def fetch(k):
        rows = pl.ds(pl.multiple_of(k * K_CHUNK, K_CHUNK), K_CHUNK)
        return [
            pltpu.make_async_copy(source.at[rows], target.at[half, k], sems.at[kind + half, k])
            for half, kind, source, target in (
                (0, 0, wq_mine, wq),
                (1, 0, wq_other, wq),
                (0, 2, wkv_mine, wkv),
                (1, 2, wkv_other, wkv),
            )
        ]

    @pl.when(step == 0)
    def _():
        for k in range(AHEAD):
            for copy in fetch(k):
                copy.start()

    @pl.when(step + AHEAD < steps)
    def _():
        for copy in fetch(step + AHEAD):
            copy.start()

    for copy in fetch(step):
        copy.wait()
    far = jnp.where(step < steps // 2, far_a[...], far_b[...])
    x = jnp.concatenate([own[...], over_a[...], over_b[...], far], axis=0)

    @pl.when(step == 0)
    def _():
        acc_q[...] = jnp.zeros_like(acc_q)
        acc_kv[...] = jnp.zeros_like(acc_kv)

    for half in range(2):
        acc_q[:, half * 512 : half * 512 + 512] += jnp.dot(
            x, wq[half, step], preferred_element_type=jnp.float32
        )
    both = jnp.concatenate([wkv[0, step], wkv[1, step]], axis=1)
    acc_kv[...] += jnp.dot(x, both, preferred_element_type=jnp.float32)

    @pl.when(step == steps - 1)
    def _():
        cos = cosine[...]
        sin = sine[...]

        def turn(u):
            return u * cos + pltpu.roll(u, HD // 2, 1) * sin

        for head in range(8):
            query[head] = turn(acc_q[:, head * HD : head * HD + HD]).astype(jnp.bfloat16)
        first = flag[...] == 0
        mine = acc_kv[:, :HD]
        other = acc_kv[:, HD:]
        low = jnp.where(first, mine, other)
        high = jnp.where(first, other, mine)
        lower = lax.broadcasted_iota(jnp.int32, (ROWS, HD), 1) < HD // 2
        keys = jnp.where(lower, low, pltpu.roll(high, HD // 2, 1))
        values = jnp.where(lower, pltpu.roll(low, HD // 2, 1), high)
        keys = keys.astype(jnp.bfloat16).astype(jnp.float32)
        kv[0] = turn(keys).astype(jnp.bfloat16)
        kv[1] = values.astype(jnp.bfloat16)


def lane_spec(start, width, chunk):
    first = start // chunk
    count = width // chunk
    return pl.BlockSpec(
        (ROWS // 2, chunk), lambda k, *_: (0, jnp.clip(k - first, 0, count - 1))
    )


def project(which, pieces, weights, cosine, sine, flag, after):
    steps = D // K_CHUNK
    near = pl.BlockSpec((PIECE, K_CHUNK), lambda k: (0, k))
    specs = [near, near, near]
    specs.append(pl.BlockSpec((PIECE, K_CHUNK), lambda k: (0, jnp.minimum(k, steps // 2 - 1))))
    specs.append(pl.BlockSpec((PIECE, K_CHUNK), lambda k: (0, jnp.maximum(k - steps // 2, 0))))
    for w in weights:
        specs.append(HBM)
    table = pl.BlockSpec((None, ROWS, HD), lambda k: (which, 0, 0))
    specs += [table, table, full_spec(flag.shape)] + [ANY] * len(after)
    return pl.pallas_call(
        project_kernel,
        out_shape=(bf16(8, ROWS, HD), bf16(2, ROWS, HD)),
        grid=(steps,),
        in_specs=specs,
        out_specs=(
            pl.BlockSpec((8, ROWS, HD), lambda k: (0, 0, 0)),
            pl.BlockSpec((2, ROWS, HD), lambda k: (0, 0, 0)),
        ),
        scratch_shapes=[
            pltpu.VMEM((ROWS, 1024), jnp.float32),
            pltpu.VMEM((ROWS, 2 * HD), jnp.float32),
            pltpu.VMEM((2, steps, K_CHUNK, 512), jnp.bfloat16),
            pltpu.VMEM((2, steps, K_CHUNK, HD), jnp.bfloat16),
            pltpu.SemaphoreType.DMA((4, steps)),
        ],
        compiler_params=params(52),
        cost_estimate=cost(PROJECT_COST[which]),
        name="project",
    )(*pieces, *weights, cosine, sine, flag, *after)


def attend_kernel(blocks, order, lanes, scalars, query, cache, q_place, k_place, *refs):
    windows = refs[:blocks]
    weights = refs[blocks : blocks + 2]
    count = 2 * len(lanes)
    outs = refs[-5 - count : -5]
    token, raw, attended, wo, sems = refs[-5:]
    step = pl.program_id(0)

    def fetch(n, half):
        return pltpu.make_async_copy(
            weights[half].at[:, pl.ds(pl.multiple_of(n * N_CHUNK, N_CHUNK), N_CHUNK)],
            wo.at[n, pl.ds(half * 512, 512), :],
            sems.at[n, half],
        )

    @pl.when(step == 0)
    def _():
        for n in range(D // N_CHUNK):
            fetch(n, 0).start()
            fetch(n, 1).start()
        token[...] = jnp.zeros((8, 128), jnp.float32)
        scale = math.log2(math.e) / math.sqrt(HD)
        slot = lax.broadcasted_iota(jnp.int32, (1, CACHE), 1)
        cache_bias = jnp.where(slot < scalars[1], 0.0, -1e30)
        causal_bias = jnp.where(k_place[...] <= q_place[...], 0.0, -1e30)
        keys = jnp.concatenate([cache[0]] + [w[c, 0] for w in windows for c in range(2)], axis=0)
        values = jnp.concatenate([cache[1]] + [w[c, 1] for w in windows for c in range(2)], axis=0)
        before = CACHE + (blocks - 1) * BLOCK
        for head in range(8):
            scores = lax.dot_general(
                query[head], keys, (((1,), (1,)), ((), ())), preferred_element_type=jnp.float32
            )
            parts = [scores[:, :CACHE] + cache_bias]
            if blocks > 1:
                parts.append(scores[:, CACHE:before])
            parts.append(scores[:, before:] + causal_bias)
            scores = jnp.concatenate(parts, axis=1)
            top = jnp.max(scores, axis=1, keepdims=True)
            grown = jnp.exp2((scores - top) * scale)
            total = jnp.sum(grown, axis=1, keepdims=True)
            out = jnp.dot(grown.astype(jnp.bfloat16), values, preferred_element_type=jnp.float32)
            raw[:, head * HD : head * HD + HD] = out / total
        for lane, (_, _, target) in enumerate(lanes):
            places = reorder(order, target)
            rows = [raw[p * SHARD : p * SHARD + SHARD] for p in places]
            attended[lane] = jnp.concatenate(rows, axis=0).astype(jnp.bfloat16)

    fetch(step, 0).wait()
    fetch(step, 1).wait()
    for lane, (start, width, _) in enumerate(lanes):
        first, last = start // N_CHUNK, (start + width) // N_CHUNK - 1

        @pl.when(jnp.logical_and(step >= first, step <= last))
        def _(lane=lane):
            term = jnp.dot(attended[lane], wo[step], preferred_element_type=jnp.float32)
            term = term.astype(jnp.bfloat16)
            outs[2 * lane][...] = term[: ROWS // 2]
            outs[2 * lane + 1][...] = term[ROWS // 2 :]


def attend(order, lanes, scalars, query, cache, q_place, k_place, windows, wo, after):
    steps = D // N_CHUNK
    blocks = len(windows)
    whole = lambda a: pl.BlockSpec(a.shape, lambda n, s: (0,) * a.ndim)
    specs = [
        whole(query),
        pl.BlockSpec((2, CACHE, HD), lambda n, s: (0, 0, s[0])),
        whole(q_place),
        whole(k_place),
        *[whole(w) for w in windows],
        HBM,
        HBM,
        *[ANY] * len(after),
    ]
    out_shape = []
    out_specs = []
    for start, width, _ in lanes:
        out_shape += [bf16(ROWS // 2, width)] * 2
        out_specs += [lane_spec(start, width, N_CHUNK)] * 2
    *results, token = pl.pallas_call(
        functools.partial(attend_kernel, blocks, order, lanes),
        out_shape=(*out_shape, f32(8, 128)),
        grid_spec=pltpu.PrefetchScalarGridSpec(
            num_scalar_prefetch=1,
            grid=(steps,),
            in_specs=specs,
            out_specs=(*out_specs, pl.BlockSpec((8, 128), lambda n, s: (0, 0))),
            scratch_shapes=[
                pltpu.VMEM((ROWS, 1024), jnp.float32),
                pltpu.VMEM((len(lanes), ROWS, 1024), jnp.bfloat16),
                pltpu.VMEM((steps, 1024, N_CHUNK), jnp.bfloat16),
                pltpu.SemaphoreType.DMA((steps, 2)),
            ],
        ),
        compiler_params=params(52),
        cost_estimate=cost(ATTEND_COST[blocks - 1]),
        name="attend",
    )(scalars, query, cache, q_place, k_place, *windows, *wo, *after)
    return results[0::2], results[1::2], (token,)


def shards(incoming, norm_gain, w_query, w_key_value, w_out, kv_cache, offsets):
    index = lax.axis_index("tensor")
    core = index % 2
    z = index // 2 % NZ
    y = index // (2 * NZ)
    head = index // 2
    offset = offsets[0, 0]
    handed = []
    beside = []
    for b in range(3):
        handed.append((from_behind(incoming[0, b : b + 1]), 0))
        beside.append((from_behind(incoming[0, b : b + 1], 1), 0))
    pairs = [[i, i + 1] for i in range(0, 4 * NZ, 2)]
    share = lambda a: lax.all_gather(a, "tensor", axis_index_groups=pairs)
    wkv = w_key_value[0].reshape(D, 2 * w_key_value.shape[3])
    wq_other = move(w_query[0], dc=1)
    wkv_other = move(wkv, dc=1)
    wo_other = move(w_out[0], dc=1)
    weights = (w_query[0], wq_other, wkv, wkv_other)
    arrived = (wq_other[:8, :128], wkv_other[:8, :128])
    flag = jnp.full((1, HD), core, jnp.int32)

    within = jnp.arange(SHARD, dtype=jnp.int32)
    freq = 500000.0 ** (-jnp.arange(HD // 2, dtype=jnp.float32) * 2.0 / HD)
    def places(c):
        moves = [steps_to(ORDER_IN, block) for block in range(8)]
        return jnp.concatenate(
            [tensor_index(y ^ dy, z ^ dz, c) * SHARD + within for dy, dz in moves]
        )

    mine = places(core)
    q_place = mine[:, None]
    k_place = jnp.concatenate([places(0), places(1)])[None, :]
    position = (offsets[0][:, None] + mine[None, :]).astype(jnp.float32)
    angle = position[:, :, None] * freq
    cos = jnp.cos(angle)
    sin = jnp.sin(angle)
    cosines = jnp.concatenate([cos, cos], axis=2)
    sines = jnp.concatenate([-sin, sin], axis=2)
    scalars = jnp.stack([head, offset])
    cache = kv_cache[0]

    held = [None] * 3
    sent = [None] * 3
    queries = [None] * 3
    windows = []
    results = [None] * 3

    def send(b, lanes, values, bit):
        sent[b] = [move(a, lane[2][bit]) for a, lane in zip(values, lanes)]

    own = [None] * 3
    near = [None] * 3
    far = [None] * 3

    def start_block(b, after):
        (own[b],), token = norm(handed[b], beside[b], norm_gain, after)
        near[b] = (move(own[b], A), move(own[b], B))
        return token

    def grow(b, after):
        (over_a, over_b), token = parts(*near[b], after)
        far[b] = (move(over_a, B), move(over_b, A))
        return token

    def project_block(b, after):
        pieces = (own[b], *near[b], *far[b])
        queries[b], kv = project(b, pieces, weights, cosines, sines, flag, after)
        windows.append(share(kv))
        return (kv,)

    def attend_block(b, after):
        held[b], given, token = attend(
            ORDER_IN,
            SCATTER[b],
            scalars,
            queries[b],
            cache,
            q_place,
            k_place,
            tuple(windows[: b + 1]),
            (w_out[0], wo_other),
            after,
        )
        send(b, SCATTER[b], given, 2)
        return token

    def shrink(b, bit, after):
        base = handed[b] if bit == 0 else None
        held[b], given, token = halve(held[b], sent[b], after, base, SCATTER[b])
        send(b, SCATTER[b], given, bit)
        if bit == 0:
            results[b] = jnp.concatenate(
                [
                    (a + r.astype(jnp.float32)).astype(jnp.bfloat16)
                    for a, r in zip(held[b], sent[b])
                ],
                axis=1,
            )
        return token

    t = start_block(0, (cosines, sines, scalars, q_place, k_place, *arrived))
    t = grow(0, (*t, wo_other[:8, :128]))
    t = start_block(1, t)
    t = project_block(0, t)
    t = grow(1, t)
    t = start_block(2, t)
    t = attend_block(0, t)
    t = project_block(1, t)
    t = grow(2, t)
    t = attend_block(1, t)
    t = shrink(0, 1, t)
    t = project_block(2, t)
    t = shrink(1, 1, t)
    t = shrink(0, 0, t)
    t = attend_block(2, t)
    t = shrink(1, 0, t)
    t = shrink(2, 1, t)
    t = shrink(2, 0, t)
    return jnp.stack(results)[None]


def solution(mesh):
    placed = (
        P("section", None, "tensor", None),
        P("section", None),
        P("section", None, "tensor"),
        P("section", None, None, "tensor"),
        P("section", "tensor", None),
        P("section", None, None, None),
        P("section", None),
    )
    return jax.shard_map(
        shards,
        mesh=mesh,
        in_specs=placed,
        out_specs=P("section", None, "tensor", None),
        check_vma=False,
    )
```
